32 devices in a mesh: tm: 4 (over y, x), space: 8 (over z, core).
Axes of the slice: x: 2, y: 2, z: 4, core: 2. Of those that a mesh axis runs over, the one named last changes fastest.
Arguments:
- video: bfloat16 [2, 8, 16, 48, 384], P(None, 'tm', 'space'), may hold values from -6 to 6
- conv_weight: bfloat16 [10368, 384], replicated, may hold values from -0.0625 to 0.0625
- norm_gain: bfloat16 [384], replicated, may hold values from 0.099609375 to 1.8984375
- down_weight: bfloat16 [3456, 384], replicated, may hold values from -0.109375 to 0.109375
- clip_lengths: int32 [2], replicated, may hold values from 1 to 8, as said below
- cotangent: bfloat16 [2, 8, 8, 24, 384], P(None, 'tm', 'space'), may hold values from -6 to 6
Outputs:
- latent: bfloat16 [2, 8, 8, 24, 384], P(None, 'tm', 'space')
- grad_conv: float32 [3981312], P(('tm', 'space'))
- grad_down: float32 [1327104], P(('tm', 'space'))
The draws below stay inside these ranges and needn't reach their ends.
Inputs may be any that keep to these rules, and one draw needn't show every extreme that they name: `clip_lengths`: clip 0 is full, with 8 valid frames.
All inputs are finite; a program needn't handle non-finite values.
Results may differ from the reference program's by a relative error of at most 0.015.
Values may be sent and summed in bfloat16 or wider, within the bound.
A program may use at most 128 MiB of HBM per device.

```python
import jax
import jax.numpy as jnp
from jax import lax

C = 384
CLIPS = 2
W = 48
FRAMES = 8
HEIGHT = 16


def draw_clip_lengths(key, part):
    others = jax.random.randint(key, (CLIPS - 1,), 1, FRAMES + 1, dtype=jnp.int32)
    return jnp.concatenate([jnp.full((1,), FRAMES, jnp.int32), others])


def block_scale(stream_key, dims, split, low, high):
    def one(position, parts):
        draws = jax.random.uniform(jax.random.fold_in(jax.random.fold_in(stream_key, 6), position), (parts,), jnp.float32, low / len(split), high / len(split))
        return jnp.repeat(jnp.exp(draws), dims[position] // parts).reshape((-1,) + (1,) * (len(dims) - position - 1))

    gain = one(*split[0])
    for cut in split[1:]:
        gain = gain * one(*cut)
    return gain


def scatter_about(rng, shape, scale, bound, shards=(), kind=jnp.bfloat16):
    values = jax.random.normal(rng, shape, jnp.float32) * scale
    if len(shards) > 0:
        values = block_scale(rng, shape, shards, -0.22, 0.18) * values
    return jnp.clip(values, min=-bound, max=bound).astype(kind)


def setup_inputs(seed: int = 0) -> dict:
    key_of = jax.random.split(jax.random.key(seed), 7)
    video = scatter_about(key_of[0], (CLIPS, FRAMES, HEIGHT, W, C), 1.0, 6.0, ((1, 4), (2, 8)))
    conv_weight = scatter_about(key_of[1], (27 * C, C), (27 * C) ** -0.5, 0.0625)
    norm_gain = jnp.clip(1.0 + 0.18 * jax.random.normal(key_of[2], (C,), jnp.float32), 0.099609375, 1.8984375).astype(jnp.bfloat16)
    down_weight = scatter_about(key_of[3], (9 * C, C), (9 * C) ** -0.5, 0.109375)
    clip_lengths = draw_clip_lengths(jax.random.fold_in(key_of[6], 71), 0)
    cotangent = scatter_about(key_of[5], (CLIPS, FRAMES, HEIGHT // 2, W // 2, C), 1.0, 6.0, ((1, 4), (2, 8)))
    return {"video": video, "conv_weight": conv_weight, "norm_gain": norm_gain, "down_weight": down_weight, "clip_lengths": clip_lengths, "cotangent": cotangent}


EPSILON = 1e-06

def norm_act(conv_out, norm_gain, keeper):
    scale = lax.rsqrt(lax.optimization_barrier(jnp.mean(conv_out * conv_out, axis=-1, keepdims=True)) + EPSILON)
    normed = conv_out * scale * norm_gain.astype(jnp.float32)
    return (normed * jax.nn.sigmoid(normed) * keeper).astype(jnp.bfloat16)

def norm_back(conv_out, norm_gain, keeper, upstream):
    scale = lax.rsqrt(lax.optimization_barrier(jnp.mean(conv_out * conv_out, axis=-1, keepdims=True)) + EPSILON)
    unit = conv_out * scale
    gained = norm_gain.astype(jnp.float32)
    normed = unit * gained
    sigma = jax.nn.sigmoid(normed)
    d_normed = upstream * keeper * sigma * (1.0 + normed * (1.0 - sigma))
    d_unit = d_normed * gained
    return (scale * (d_unit - unit * lax.optimization_barrier(jnp.mean(d_unit * unit, axis=-1, keepdims=True)))).astype(jnp.bfloat16)

def conv_window(padded, tap, frames, rows, start):
    width = padded.shape[3] - 2
    frame_tap = tap // 9
    row_tap = tap // 3 % 3
    col_tap = tap % 3
    return padded[:, frame_tap:frame_tap + frames, start + row_tap:start + row_tap + rows, col_tap:col_tap + width]

def causal_conv(padded, conv_weight, frames, rows, start):
    channels = padded.shape[-1]
    width = padded.shape[3] - 2
    shape = (padded.shape[0], frames, rows, width, channels)
    total = jnp.zeros(shape, jnp.float32)
    for tap in range(27):
        window = conv_window(padded, tap, frames, rows, start).reshape(-1, channels)
        block = conv_weight[tap * channels:(tap + 1) * channels]
        total = total + jnp.dot(window, block, preferred_element_type=jnp.float32).reshape(shape)
    return total

def conv_weight_grad(padded, d_conv, frames, rows, start):
    channels = padded.shape[-1]
    flat_grad = d_conv.reshape(-1, channels)
    blocks = []
    for tap in range(27):
        window = conv_window(padded, tap, frames, rows, start).reshape(-1, channels)
        blocks.append(jnp.dot(window.T, flat_grad, preferred_element_type=jnp.float32))
    return jnp.stack(blocks).reshape(-1)

def down_window(hpad, tap):
    out_rows = (hpad.shape[2] - 1) // 2
    out_cols = (hpad.shape[3] - 1) // 2
    row_tap = tap // 3
    col_tap = tap % 3
    return hpad[:, :, row_tap:row_tap + 2 * out_rows:2, col_tap:col_tap + 2 * out_cols:2]

def down_forward(hpad, down_weight):
    channels = hpad.shape[-1]
    shape = (hpad.shape[0], hpad.shape[1], (hpad.shape[2] - 1) // 2, (hpad.shape[3] - 1) // 2, channels)
    total = jnp.zeros(shape, jnp.float32)
    for tap in range(9):
        window = down_window(hpad, tap).reshape(-1, channels)
        block = down_weight[tap * channels:(tap + 1) * channels]
        total = total + jnp.dot(window, block, preferred_element_type=jnp.float32).reshape(shape)
    return total

def down_weight_grad(hpad, cotangent):
    channels = hpad.shape[-1]
    flat_cot = cotangent.reshape(-1, channels)
    blocks = []
    for tap in range(9):
        window = down_window(hpad, tap).reshape(-1, channels)
        blocks.append(jnp.dot(window.T, flat_cot, preferred_element_type=jnp.float32))
    return jnp.stack(blocks).reshape(-1)

def down_back(hpad_shape, cotangent, down_weight):
    channels = cotangent.shape[-1]
    out_rows = cotangent.shape[2]
    out_cols = cotangent.shape[3]
    flat_cot = cotangent.reshape(-1, channels)
    d_pad = jnp.zeros(hpad_shape, jnp.float32)
    for tap in range(9):
        row_tap = tap // 3
        col_tap = tap % 3
        block = down_weight[tap * channels:(tap + 1) * channels]
        piece = jnp.dot(flat_cot, block.T, preferred_element_type=jnp.float32).reshape(cotangent.shape)
        d_pad = d_pad.at[:, :, row_tap:row_tap + 2 * out_rows:2, col_tap:col_tap + 2 * out_cols:2].add(piece)
    return d_pad

def reference(video, conv_weight, norm_gain, down_weight, clip_lengths, cotangent):
    frames = video.shape[1]
    rows = video.shape[2]
    width = video.shape[3]
    keeper = (jnp.arange(frames, dtype=jnp.int32)[None, :] < clip_lengths[:, None]).astype(jnp.float32)
    keeper = keeper[:, :, None, None, None]
    masked = video * keeper.astype(jnp.bfloat16)
    padded = jnp.pad(masked, ((0, 0), (2, 0), (1, 1), (1, 1), (0, 0)))
    conv_out = causal_conv(padded, conv_weight, frames, rows, 0)
    hidden = norm_act(conv_out, norm_gain, keeper)
    hpad = jnp.pad(hidden, ((0, 0), (0, 0), (0, 1), (0, 1), (0, 0)))
    latent = down_forward(hpad, down_weight).astype(jnp.bfloat16)
    grad_down = down_weight_grad(hpad, cotangent)
    d_hidden = down_back(hpad.shape, cotangent, down_weight)[:, :, :rows, :width]
    d_conv = norm_back(conv_out, norm_gain, keeper, d_hidden)
    grad_conv = conv_weight_grad(padded, d_conv, frames, rows, 0)
    return (latent, grad_conv, grad_down)
```

```python
import jax
import jax.numpy as jnp
from jax import lax
from jax.sharding import PartitionSpec as P

EPSILON = 1e-06
F32 = jnp.float32
BF16 = jnp.bfloat16


def shifted(array, axis, by):
    count = lax.axis_size(axis)
    pairs = [(i, i + by) for i in range(count) if 0 <= i + by < count]
    return lax.ppermute(array, axis, pairs)


def pad_dim(array, dim, before, after):
    widths = [(0, 0)] * array.ndim
    widths[dim] = (before, after)
    return jnp.pad(array, widths)


def exchange(array, dim, axis, bit):
    mine = (lax.axis_index(axis) >> bit) & 1
    pairs = [(i, i ^ (1 << bit)) for i in range(lax.axis_size(axis))]
    sent = lax.dynamic_index_in_dim(array, 1 - mine, dim, keepdims=False)
    kept = lax.dynamic_index_in_dim(array, mine, dim, keepdims=False)
    got = lax.ppermute(sent, axis, pairs)
    return kept.astype(F32) + got.astype(F32)


def halving(array, order):
    left = [("tm", b) for b in reversed(range(lax.axis_size("tm").bit_length() - 1))]
    left += [("space", b) for b in reversed(range(lax.axis_size("space").bit_length() - 1))]
    for step, (axis, bit) in enumerate(order):
        dim = left.index((axis, bit))
        left.pop(dim)
        array = exchange(array, dim, axis, bit)
        if step + 1 < len(order):
            array = array.astype(BF16)
    return array


def local(video, conv_weight, norm_gain, down_weight, clip_lengths, cotangent):
    clips, frames, rows, width, channels = video.shape
    out_rows = cotangent.shape[2]
    half = width // 2
    tm, space = lax.axis_size("tm"), lax.axis_size("space")
    devices = tm * space
    frame_ids = lax.axis_index("tm") * frames + jnp.arange(frames, dtype=jnp.int32)
    keeper = (frame_ids[None, :] < clip_lengths[:, None]).astype(F32)[:, :, None, None, None, None]

    split = video.reshape(clips, frames, rows, half, 2, channels)
    masked = jnp.stack([split[..., 0, :], split[..., 1, :]], axis=3) * keeper.astype(BF16)
    earlier = shifted(masked, "tm", 1)
    joined = jnp.concatenate([earlier, masked], axis=1)
    above = shifted(joined[:, :, rows - 1 :], "space", 1)
    under = shifted(joined[:, :, :1], "space", -1)
    tall = jnp.concatenate([above, joined, under], axis=2)
    even, odd = tall[:, :, :, 0], tall[:, :, :, 1]
    odd_before = pad_dim(odd, 3, 1, 0)[:, :, :, :half]
    even_after = pad_dim(even, 3, 0, 1)[:, :, :, 1:]
    wide = jnp.stack(
        [
            jnp.concatenate([odd_before, even, odd], axis=-1),
            jnp.concatenate([even, odd, even_after], axis=-1),
        ],
        axis=3,
    )
    windows = jnp.concatenate(
        [wide[:, dt : dt + frames, dr : dr + rows] for dt in range(3) for dr in range(3)], axis=-1
    ).reshape(-1, 27 * channels)

    cot = cotangent.reshape(-1, channels)
    pieces = lax.dot_general(
        cot, down_weight, (((1,), (1,)), ((), ())), preferred_element_type=F32
    ).reshape(clips, frames, out_rows, half, 9, channels)

    def row_part(dr):
        first, second, third = (pieces[..., 3 * dr + dc, :] for dc in range(3))
        moved = pad_dim(third, 3, 1, 0)[:, :, :, :half]
        return jnp.stack([first + moved, second], axis=3)

    top, middle, low = (row_part(dr) for dr in range(3))
    carried = shifted(low[:, :, out_rows - 1 :].astype(BF16), "space", 1).astype(F32)
    top = top + jnp.concatenate([carried, low[:, :, : out_rows - 1]], axis=2)
    upstream = jnp.stack([top, middle], axis=3).reshape(clips, frames, rows, 2, half, channels)

    conv_out = jnp.dot(windows, conv_weight, preferred_element_type=F32).reshape(
        clips, frames, rows, 2, half, channels
    )
    scale = lax.rsqrt(jnp.mean(conv_out * conv_out, axis=-1, keepdims=True) + EPSILON)
    gained = norm_gain.astype(F32)
    unit = conv_out * scale
    normed = unit * gained
    sigma = jax.nn.sigmoid(normed)
    hidden = (normed * sigma * keeper).astype(BF16)
    below = shifted(hidden[:, :, :1], "space", -1)

    d_unit = upstream * keeper * sigma * (1.0 + normed * (1.0 - sigma)) * gained
    d_conv = (scale * (d_unit - unit * jnp.mean(d_unit * unit, axis=-1, keepdims=True))).astype(BF16)
    grad_conv = lax.dot_general(
        windows,
        d_conv.reshape(-1, channels),
        (((0,), (0,)), ((), ())),
        preferred_element_type=F32,
    ).astype(BF16)

    conv_rows = 27 * channels // devices
    down_rows = 9 * channels // devices
    cut = (conv_rows + down_rows) // 2
    bits_tm, bits_space = tm.bit_length() - 1, space.bit_length() - 1
    lead = (2,) * (bits_tm + bits_space)
    by_device = grad_conv.reshape(devices, conv_rows, channels)
    core = [("space", 0)]
    along = [("space", b) for b in range(1, bits_space)]
    plane = [("tm", b) for b in range(bits_tm)]
    first = by_device[:, :cut].reshape(*lead, cut, channels)
    first = halving(first, core + plane + along)

    tall_hidden = jnp.concatenate([hidden, below], axis=2)
    left, right = tall_hidden[:, :, :, 0], tall_hidden[:, :, :, 1]
    left_after = pad_dim(left, 3, 0, 1)[:, :, :, 1:]
    columns = jnp.concatenate([left, right, left_after], axis=-1)
    down_windows = jnp.concatenate(
        [columns[:, :, dr : dr + 2 * out_rows : 2] for dr in range(3)], axis=-1
    ).reshape(-1, 9 * channels)
    grad_down = lax.dot_general(
        down_windows, cot, (((0,), (0,)), ((), ())), preferred_element_type=F32
    ).astype(BF16)
    second = jnp.concatenate(
        [by_device[:, cut:], grad_down.reshape(devices, down_rows, channels)], axis=1
    ).reshape(*lead, conv_rows + down_rows - cut, channels)
    second = halving(second, core + plane[::-1] + along)
    latent = jnp.dot(down_windows, down_weight, preferred_element_type=F32).astype(BF16)

    return (
        latent.reshape(clips, frames, out_rows, half, channels),
        jnp.concatenate([first, second[: conv_rows - cut]], axis=0).reshape(-1),
        second[conv_rows - cut :].reshape(-1),
    )


def solution(mesh):
    in_specs = (
        P(None, "tm", "space", None, None),
        P(),
        P(),
        P(),
        P(),
        P(None, "tm", "space", None, None),
    )
    out_specs = (P(None, "tm", "space", None, None), P(("tm", "space")), P(("tm", "space")))
    return jax.shard_map(local, mesh=mesh, in_specs=in_specs, out_specs=out_specs, check_vma=False)
```

```python
import jax
import jax.numpy as jnp
from jax import lax
from jax.sharding import PartitionSpec as P

EPSILON = 1e-06
F32 = jnp.float32
BF16 = jnp.bfloat16


def shifted(array, axis, by):
    count = lax.axis_size(axis)
    pairs = [(i, i + by) for i in range(count) if 0 <= i + by < count]
    return lax.ppermute(array, axis, pairs)


def pad_dim(array, dim, before, after):
    widths = [(0, 0)] * array.ndim
    widths[dim] = (before, after)
    return jnp.pad(array, widths)


def partner_of(axis, bit):
    return [(i, i ^ (1 << bit)) for i in range(lax.axis_size(axis))]


def halving(array, left, order):
    left = list(left)
    for axis, bit in order:
        dim = left.index((axis, bit))
        left.pop(dim)
        mine = (lax.axis_index(axis) >> bit) & 1
        sent = lax.dynamic_index_in_dim(array, 1 - mine, dim, keepdims=False)
        kept = lax.dynamic_index_in_dim(array, mine, dim, keepdims=False)
        got = lax.ppermute(sent, axis, partner_of(axis, bit))
        array = kept.astype(F32) + got.astype(F32)
        if left:
            array = array.astype(BF16)
    return array


def local(video, conv_weight, norm_gain, down_weight, clip_lengths, cotangent):
    clips, frames, rows, width, channels = video.shape
    out_rows = cotangent.shape[2]
    half = width // 2
    tm, space = lax.axis_size("tm"), lax.axis_size("space")
    devices = tm * space
    frame_ids = lax.axis_index("tm") * frames + jnp.arange(frames, dtype=jnp.int32)
    keeper = (frame_ids[None, :] < clip_lengths[:, None]).astype(F32)[:, :, None, None, None, None]

    split = video.reshape(clips, frames, rows, half, 2, channels)
    masked = jnp.stack([split[..., 0, :], split[..., 1, :]], axis=3) * keeper.astype(BF16)
    earlier = shifted(masked, "tm", 1)
    joined = jnp.concatenate([earlier, masked], axis=1)
    above = shifted(joined[:, :, rows - 1 :], "space", 1)
    under = shifted(joined[:, :, :1], "space", -1)
    tall = jnp.concatenate([above, joined, under], axis=2)
    even, odd = tall[:, :, :, 0], tall[:, :, :, 1]
    odd_before = pad_dim(odd, 3, 1, 0)[:, :, :, :half]
    even_after = pad_dim(even, 3, 0, 1)[:, :, :, 1:]
    wide = jnp.stack(
        [
            jnp.concatenate([odd_before, even, odd], axis=-1),
            jnp.concatenate([even, odd, even_after], axis=-1),
        ],
        axis=3,
    )
    windows = jnp.concatenate(
        [wide[:, dt : dt + frames, dr : dr + rows] for dt in range(3) for dr in range(3)], axis=-1
    ).reshape(-1, 27 * channels)

    cot = cotangent.reshape(-1, channels)
    pieces = lax.dot_general(
        cot, down_weight, (((1,), (1,)), ((), ())), preferred_element_type=F32
    ).reshape(clips, frames, out_rows, half, 9, channels)

    def row_part(dr):
        first, second, third = (pieces[..., 3 * dr + dc, :] for dc in range(3))
        moved = pad_dim(third, 3, 1, 0)[:, :, :, :half]
        return jnp.stack([first + moved, second], axis=3)

    top, middle, low = (row_part(dr) for dr in range(3))
    carried = shifted(low[:, :, out_rows - 1 :].astype(BF16), "space", 1).astype(F32)
    top = top + jnp.concatenate([carried, low[:, :, : out_rows - 1]], axis=2)
    upstream = jnp.stack([top, middle], axis=3).reshape(clips, frames, rows, 2, half, channels)

    conv_out = jnp.dot(windows, conv_weight, preferred_element_type=F32).reshape(
        clips, frames, rows, 2, half, channels
    )
    scale = lax.rsqrt(jnp.mean(conv_out * conv_out, axis=-1, keepdims=True) + EPSILON)
    gained = norm_gain.astype(F32)
    unit = conv_out * scale
    normed = unit * gained
    sigma = jax.nn.sigmoid(normed)
    hidden = (normed * sigma * keeper).astype(BF16)
    below = shifted(hidden[:, :, :1], "space", -1)

    d_unit = upstream * keeper * sigma * (1.0 + normed * (1.0 - sigma)) * gained
    d_conv = (scale * (d_unit - unit * jnp.mean(d_unit * unit, axis=-1, keepdims=True))).astype(BF16)
    grad_conv = lax.dot_general(
        windows,
        d_conv.reshape(-1, channels),
        (((0,), (0,)), ((), ())),
        preferred_element_type=F32,
    ).astype(BF16)

    tall_hidden = jnp.concatenate([hidden, below], axis=2)
    even, odd = tall_hidden[:, :, :, 0], tall_hidden[:, :, :, 1]
    even_after = pad_dim(even, 3, 0, 1)[:, :, :, 1:]
    columns = jnp.concatenate([even, odd, even_after], axis=-1)
    down_windows = jnp.concatenate(
        [columns[:, :, dr : dr + 2 * out_rows : 2] for dr in range(3)], axis=-1
    ).reshape(-1, 9 * channels)
    grad_down = lax.dot_general(
        down_windows, cot, (((0,), (0,)), ((), ())), preferred_element_type=F32
    ).astype(BF16)
    latent = jnp.dot(down_windows, down_weight, preferred_element_type=F32).astype(BF16)

    conv_rows = 27 * channels // devices
    down_rows = 9 * channels // devices
    total_rows = conv_rows + down_rows
    bits_tm, bits_space = tm.bit_length() - 1, space.bit_length() - 1
    plane = [("tm", b) for b in range(bits_tm)]
    along = [("space", b) for b in range(1, bits_space)]
    orders = [plane + along, plane[::-1] + along, along[:1] + plane + along[1:]]
    left = [("tm", b) for b in reversed(range(bits_tm))]
    left += [("space", b) for b in reversed(range(1, bits_space))]
    lead = (2,) * len(left)
    core = lax.axis_index("space") & 1
    conv_pairs = grad_conv.reshape(devices // 2, 2 * conv_rows, channels)
    down_pairs = grad_down.reshape(devices // 2, 2 * down_rows, channels)

    def core_half(which, columns):
        return jnp.concatenate(
            [
                jnp.where(which == 1, pairs[:, count:, columns], pairs[:, :count, columns])
                for pairs, count in ((conv_pairs, conv_rows), (down_pairs, down_rows))
            ],
            axis=1,
        )

    parts = []
    wide_of = channels // len(orders)
    for index, order in enumerate(orders):
        columns = slice(index * wide_of, (index + 1) * wide_of)
        got = lax.ppermute(core_half(1 - core, columns), "space", partner_of("space", 0))
        part = (core_half(core, columns).astype(F32) + got.astype(F32)).astype(BF16)
        parts.append(halving(part.reshape(*lead, total_rows, wide_of), left, order))
    reduced = jnp.concatenate(parts, axis=-1)

    return (
        latent.reshape(clips, frames, out_rows, half, channels),
        reduced[:conv_rows].reshape(-1),
        reduced[conv_rows:].reshape(-1),
    )


def solution(mesh):
    in_specs = (
        P(None, "tm", "space", None, None),
        P(),
        P(),
        P(),
        P(),
        P(None, "tm", "space", None, None),
    )
    out_specs = (P(None, "tm", "space", None, None), P(("tm", "space")), P(("tm", "space")))
    return jax.shard_map(local, mesh=mesh, in_specs=in_specs, out_specs=out_specs, check_vma=False)
```

```python
import jax
import jax.numpy as jnp
from jax import lax
from jax.sharding import PartitionSpec as P

EPSILON = 1e-06
F32 = jnp.float32
BF16 = jnp.bfloat16


def shifted(array, axis, by):
    count = lax.axis_size(axis)
    pairs = [(i, i + by) for i in range(count) if 0 <= i + by < count]
    return lax.ppermute(array, axis, pairs)


def pad_dim(array, dim, before, after):
    widths = [(0, 0)] * array.ndim
    widths[dim] = (before, after)
    return jnp.pad(array, widths)


def partner_of(axis, bit):
    return [(i, i ^ (1 << bit)) for i in range(lax.axis_size(axis))]


def halving(array, left, order):
    left = list(left)
    space_bits = lax.axis_size("space").bit_length() - 1
    devices = lax.axis_size("tm") * lax.axis_size("space")
    for axis, bit in order[:-2]:
        dim = left.index((axis, bit))
        left.pop(dim)
        mine = (lax.axis_index(axis) >> bit) & 1
        sent = lax.dynamic_index_in_dim(array, 1 - mine, dim, keepdims=False)
        kept = lax.dynamic_index_in_dim(array, mine, dim, keepdims=False)
        got = lax.ppermute(sent, axis, partner_of(axis, bit))
        array = (kept.astype(F32) + got.astype(F32)).astype(BF16)
    slow, fast = ((lax.axis_index(axis) >> bit) & 1 for axis, bit in left)
    masks = [1 << (bit + (space_bits if axis == "tm" else 0)) for axis, bit in left]
    blocks = array.reshape(4, *array.shape[2:])
    total = lax.dynamic_index_in_dim(blocks, 2 * slow + fast, 0, keepdims=False).astype(F32)
    for flip in (3, 2, 1):
        sent = lax.dynamic_index_in_dim(blocks, (2 * slow + fast) ^ flip, 0, keepdims=False)
        mask = masks[0] * (flip >> 1) + masks[1] * (flip & 1)
        pairs = [(i, i ^ mask) for i in range(devices)]
        total = total + lax.ppermute(sent, ("tm", "space"), pairs).astype(F32)
    return total


def local(video, conv_weight, norm_gain, down_weight, clip_lengths, cotangent):
    clips, frames, rows, width, channels = video.shape
    out_rows = cotangent.shape[2]
    half = width // 2
    tm, space = lax.axis_size("tm"), lax.axis_size("space")
    devices = tm * space
    frame_ids = lax.axis_index("tm") * frames + jnp.arange(frames, dtype=jnp.int32)
    keeper = (frame_ids[None, :] < clip_lengths[:, None]).astype(F32)[:, :, None, None, None, None]

    split = video.reshape(clips, frames, rows, half, 2, channels)
    masked = jnp.stack([split[..., 0, :], split[..., 1, :]], axis=3) * keeper.astype(BF16)
    earlier = shifted(masked, "tm", 1)
    joined = jnp.concatenate([earlier, masked], axis=1)
    above = shifted(joined[:, :, rows - 1 :], "space", 1)
    under = shifted(joined[:, :, :1], "space", -1)
    tall = jnp.concatenate([above, joined, under], axis=2)
    even, odd = tall[:, :, :, 0], tall[:, :, :, 1]
    odd_before = pad_dim(odd, 3, 1, 0)[:, :, :, :half]
    even_after = pad_dim(even, 3, 0, 1)[:, :, :, 1:]
    wide = jnp.stack(
        [
            jnp.concatenate([odd_before, even, odd], axis=-1),
            jnp.concatenate([even, odd, even_after], axis=-1),
        ],
        axis=3,
    )
    windows = jnp.concatenate(
        [wide[:, dt : dt + frames, dr : dr + rows] for dt in range(3) for dr in range(3)], axis=-1
    ).reshape(-1, 27 * channels)

    cot = cotangent.reshape(-1, channels)
    pieces = lax.dot_general(
        cot, down_weight, (((1,), (1,)), ((), ())), preferred_element_type=F32
    ).reshape(clips, frames, out_rows, half, 9, channels)

    def row_part(dr):
        first, second, third = (pieces[..., 3 * dr + dc, :] for dc in range(3))
        moved = pad_dim(third, 3, 1, 0)[:, :, :, :half]
        return jnp.stack([first + moved, second], axis=3)

    top, middle, low = (row_part(dr) for dr in range(3))
    carried = shifted(low[:, :, out_rows - 1 :].astype(BF16), "space", 1).astype(F32)
    top = top + jnp.concatenate([carried, low[:, :, : out_rows - 1]], axis=2)
    upstream = jnp.stack([top, middle], axis=3).reshape(clips, frames, rows, 2, half, channels)

    conv_out = jnp.dot(windows, conv_weight, preferred_element_type=F32).reshape(
        clips, frames, rows, 2, half, channels
    )
    scale = lax.rsqrt(jnp.mean(conv_out * conv_out, axis=-1, keepdims=True) + EPSILON)
    gained = norm_gain.astype(F32)
    unit = conv_out * scale
    normed = unit * gained
    sigma = jax.nn.sigmoid(normed)
    hidden = (normed * sigma * keeper).astype(BF16)
    below = shifted(hidden[:, :, :1], "space", -1)

    d_unit = upstream * keeper * sigma * (1.0 + normed * (1.0 - sigma)) * gained
    d_conv = (scale * (d_unit - unit * jnp.mean(d_unit * unit, axis=-1, keepdims=True))).astype(BF16)
    grad_conv = lax.dot_general(
        windows,
        d_conv.reshape(-1, channels),
        (((0,), (0,)), ((), ())),
        preferred_element_type=F32,
    ).astype(BF16)

    tall_hidden = jnp.concatenate([hidden, below], axis=2)
    even, odd = tall_hidden[:, :, :, 0], tall_hidden[:, :, :, 1]
    even_after = pad_dim(even, 3, 0, 1)[:, :, :, 1:]
    columns = jnp.concatenate([even, odd, even_after], axis=-1)
    down_windows = jnp.concatenate(
        [columns[:, :, dr : dr + 2 * out_rows : 2] for dr in range(3)], axis=-1
    ).reshape(-1, 9 * channels)
    grad_down = lax.dot_general(
        down_windows, cot, (((0,), (0,)), ((), ())), preferred_element_type=F32
    ).astype(BF16)
    latent = jnp.dot(down_windows, down_weight, preferred_element_type=F32).astype(BF16)

    conv_rows = 27 * channels // devices
    down_rows = 9 * channels // devices
    total_rows = conv_rows + down_rows
    bits_tm, bits_space = tm.bit_length() - 1, space.bit_length() - 1
    plane = [("tm", b) for b in range(bits_tm)]
    along = [("space", b) for b in range(1, bits_space)]
    orders = [plane + along, plane[::-1] + along, along[:1] + plane + along[1:]]
    left = [("tm", b) for b in reversed(range(bits_tm))]
    left += [("space", b) for b in reversed(range(1, bits_space))]
    lead = (2,) * len(left)
    core = lax.axis_index("space") & 1
    conv_pairs = grad_conv.reshape(devices // 2, 2 * conv_rows, channels)
    down_pairs = grad_down.reshape(devices // 2, 2 * down_rows, channels)

    def core_half(pairs, count, which, columns):
        return jnp.where(which == 1, pairs[:, count:, columns], pairs[:, :count, columns])

    def core_sum(pairs, count, columns):
        sent = core_half(pairs, count, 1 - core, columns)
        got = lax.ppermute(sent, "space", partner_of("space", 0))
        return core_half(pairs, count, core, columns).astype(F32) + got.astype(F32)

    parts = []
    wide_of = channels // len(orders)
    down_sum = core_sum(down_pairs, down_rows, slice(None)).astype(BF16)
    for index, order in enumerate(orders):
        columns = slice(index * wide_of, (index + 1) * wide_of)
        conv_sum = core_sum(conv_pairs, conv_rows, columns).astype(BF16)
        part = jnp.concatenate([conv_sum, down_sum[:, :, columns]], axis=1)
        parts.append(halving(part.reshape(*lead, total_rows, wide_of), left, order))
    reduced = jnp.concatenate(parts, axis=-1)

    return (
        latent.reshape(clips, frames, out_rows, half, channels),
        reduced[:conv_rows].reshape(-1),
        reduced[conv_rows:].reshape(-1),
    )


def solution(mesh):
    in_specs = (
        P(None, "tm", "space", None, None),
        P(),
        P(),
        P(),
        P(),
        P(None, "tm", "space", None, None),
    )
    out_specs = (P(None, "tm", "space", None, None), P(("tm", "space")), P(("tm", "space")))
    return jax.shard_map(local, mesh=mesh, in_specs=in_specs, out_specs=out_specs, check_vma=False)
```
